512 devices in a mesh: ep: 32 (over x_lo, z, core), et: 16 (over x_hi, y).
Axes of the slice: x: 4 (x_hi: 2, x_lo: 2; x = x_hi * 2 + x_lo), y: 8, z: 8, core: 2. Of those that a mesh axis runs over, the one named last changes fastest.
Arguments:
- tokens: bfloat16 [8192, 2048], P('ep', 'et'), may hold values from -6 to 6
- cotangent: bfloat16 [8192, 2048], P('ep', 'et'), may hold values from -1.5 to 1.5
- w_up: bfloat16 [32, 2048, 4096], P('ep', None, 'et'), may hold values from -0.1875 to 0.1875
- w_down: bfloat16 [32, 4096, 2048], P('ep', 'et'), may hold values from -0.09375 to 0.09375
- saved_pre: bfloat16 [32, 512, 4096], P('ep', None, 'et'), may hold values from -6 to 6
- gates: float32 [32, 512], P('ep'), may hold values from 0.25 to 2
- picks: int32 [32, 32, 16], P('ep'), may hold values from 0 to 255, as said below
- counts: int32 [32, 32], P('ep'), may hold values from 4 to 16, as said below
Outputs:
- grad_tokens: bfloat16 [8192, 2048], P('ep', 'et')
- grad_up: bfloat16 [32, 2048, 4096], P('ep', None, 'et')
- grad_down: bfloat16 [32, 4096, 2048], P('ep', 'et')
- gate_grad: float32 [32, 512], P('ep')
The draws below stay inside these ranges and needn't reach their ends.
Inputs may be any that keep to these rules, and one draw needn't show every extreme that they name: For each ep index s and expert e the entries picks[s, e, :] are distinct tokens among that index's 256; slots k >= counts[s, e] are padding and are ignored. `counts`: some expert takes 16 tokens from every ep index.
All inputs are finite; a program needn't handle non-finite values.
Results may differ from the reference program's by a relative error of at most 0.0049.
Values may be sent and summed in bfloat16 or wider, within the bound.
No kernel may reach another device: no remote copies, remote signals or barrier semaphores. Data moves between devices by JAX's collectives and lax.ppermute only.
A program may use at most 64 MiB of HBM per device.

```python
import math
import jax
import jax.numpy as jnp
from jax import lax

D = 2048
HID = 4096
TOK_DEV = 256
SLOT = 16
EXPERTS = 32
TOKENS = 8192
CAP = 512
N_EP = 32


def draw_picks(key, part):
    key_list = jax.random.split(key, N_EP * EXPERTS)

    def single_pick(subkey):
        return jax.random.permutation(subkey, TOK_DEV)[:SLOT]
    return jax.vmap(single_pick)(key_list).reshape(N_EP, EXPERTS, SLOT).astype(jnp.int32)


def draw_counts(key, part):
    key_base, key_full = jax.random.split(jax.random.fold_in(key, 7))
    drawn = jax.random.randint(key_base, (N_EP, EXPERTS), max(1, SLOT // 4), SLOT + 1)
    chosen = jax.random.randint(key_full, (), 0, EXPERTS)
    chosen_mask = jnp.arange(EXPERTS, dtype=jnp.int32)[None, :] == chosen
    return jnp.where(chosen_mask, SLOT, drawn).astype(jnp.int32)


def strengthened(values, key, source, target, blocks, factor):
    owner, partner = [(jnp.arange(values.shape[dim]) // (values.shape[dim] // blocks)).reshape([-1 if axis == dim else 1 for axis in range(values.ndim)]) for dim in (source, target)]
    chosen = jax.random.permutation(key, blocks)[partner]
    strong = (owner == chosen) | (owner == (partner + blocks // 2) % blocks)
    return jnp.where(strong, factor * values, values)


def level_of(rng, dims, shards, least, largest):
    def one(position, shards_of):
        draws = jax.random.uniform(jax.random.fold_in(jax.random.fold_in(rng, 6), position), (shards_of,), jnp.float32, least / len(shards), largest / len(shards))
        return jnp.repeat(jnp.exp(draws), dims[position] // shards_of).reshape((-1,) + (1,) * (len(dims) - position - 1))

    loudness = one(*shards[0])
    for cut in shards[1:]:
        loudness = loudness * one(*cut)
    return loudness


def bell_draw(stream_key, extent, spread, limit, cuts=(), held_as=jnp.bfloat16):
    factor_of = level_of(stream_key, extent, cuts, -0.22, 0.18) if cuts else 1.0
    array = jax.random.normal(stream_key, extent, jnp.float32) * spread * factor_of
    return jnp.minimum(jnp.maximum(array, -limit), limit).astype(held_as)


def heavy_noise(stream_key, extent, deviation, most, cuts, heavy, kind=jnp.bfloat16):
    array = deviation * jax.random.normal(stream_key, extent, jnp.float32)
    if cuts:
        array = array * level_of(stream_key, extent, cuts, -0.22, 0.18)
    return jnp.clip(strengthened(array, jax.random.fold_in(stream_key, 3), *heavy), -most, most).astype(kind)


def setup_inputs(seed: int = 0) -> dict:
    arg_keys = jax.random.split(jax.random.key(seed), 9)
    return {
        "tokens": bell_draw(arg_keys[0], (TOKENS, D), 1.0, 6.0, ((0, 32), (1, 16))),
        "cotangent": bell_draw(arg_keys[1], (TOKENS, D), 0.25, 1.5, ((0, 32), (1, 16))),
        "w_up": heavy_noise(arg_keys[2], (EXPERTS, D, HID), D ** -0.5, 0.1875, ((0, 32), (2, 16)), (2, 1, 16, 2.0)),
        "w_down": bell_draw(arg_keys[3], (EXPERTS, HID, D), HID ** -0.5, 0.09375, ((0, 32), (1, 16))),
        "saved_pre": bell_draw(arg_keys[4], (EXPERTS, CAP, HID), 1.0, 6.0, ((0, 32), (2, 16))),
        "gates": jnp.clip(jnp.exp(math.log(2.0) - 2.0794415 * jax.random.uniform(arg_keys[5], (EXPERTS, CAP), jnp.float32) ** level_of(arg_keys[5], (EXPERTS, CAP), ((0, 32),), -0.2, 0.2)), 0.25, 2.0),
        "picks": draw_picks(jax.random.fold_in(arg_keys[8], 71), 0),
        "counts": draw_counts(jax.random.fold_in(arg_keys[8], 71), 0),
    }


def reference(tokens, cotangent, w_up, w_down, saved_pre, gates, picks, counts):
    slot_pos = jnp.arange(CAP, dtype=jnp.int32) % SLOT
    source_of = jnp.arange(CAP, dtype=jnp.int32) // SLOT

    def per_expert(total, expert_id):
        count_row = counts[:, expert_id]
        is_valid = slot_pos < count_row[source_of]
        local_idx = picks[:, expert_id, :].reshape(CAP).astype(jnp.int32)
        row_index = (source_of * TOK_DEV + local_idx).astype(jnp.int32)
        picked_x = jnp.where(is_valid[:, None], tokens[row_index], jnp.zeros((), tokens.dtype))
        picked_y = jnp.where(is_valid[:, None], cotangent[row_index], jnp.zeros((), cotangent.dtype))
        pre_act = saved_pre[expert_id]
        hidden = jnp.maximum(pre_act, jnp.zeros((), pre_act.dtype))
        w_first = w_up[expert_id]
        w_second = w_down[expert_id]
        back_grad = jnp.dot(picked_y, w_second.T, preferred_element_type=jnp.float32)
        expert_out = jnp.dot(hidden, w_second, preferred_element_type=jnp.float32)
        gate_term = jnp.sum(expert_out * picked_y.astype(jnp.float32), axis=1)
        gate_row = gates[expert_id]
        pre_grad = (gate_row[:, None] * back_grad * (pre_act > 0)).astype(jnp.bfloat16)
        out_grad = (gate_row[:, None] * picked_y.astype(jnp.float32)).astype(jnp.bfloat16)
        down_grad = jnp.dot(hidden.T, out_grad, preferred_element_type=jnp.float32).astype(jnp.bfloat16)
        up_grad = jnp.dot(picked_x.T, pre_grad, preferred_element_type=jnp.float32).astype(jnp.bfloat16)
        token_part = jnp.dot(pre_grad, w_first.T, preferred_element_type=jnp.float32)
        token_part = jnp.where(is_valid[:, None], token_part, jnp.zeros((), jnp.float32))
        total = total.at[row_index].add(token_part)
        return total, (up_grad, down_grad, gate_term)

    start_total = jnp.zeros((TOKENS, D), jnp.float32)
    total, (grad_up, grad_down, gate_grad) = lax.scan(per_expert, start_total, jnp.arange(EXPERTS, dtype=jnp.int32))
    return total.astype(jnp.bfloat16), grad_up, grad_down, gate_grad
```

```python
import jax
import jax.numpy as jnp
from jax import lax
from jax.experimental import pallas as pl
from jax.experimental.pallas import tpu as pltpu
from jax.sharding import Mesh, PartitionSpec as P

HI = 2
CHUNKS = 4
EXTRA = 16
NN = (((1,), (0,)), ((), ()))
NT = (((1,), (1,)), ((), ()))
TN = (((0,), (0,)), ((), ()))
VMEM_LIMIT = 56 << 20


def dot32(a, b, dims=NN):
    return lax.dot_general(a, b, dims, preferred_element_type=jnp.float32)


def pick_kernel(picks_ref, counts_ref, tokens_ref, cotangent_ref, sel_ref, out_ref):
    n_slots, n_experts = picks_ref.shape
    n_tokens = tokens_ref.shape[0]
    slot = lax.broadcasted_iota(jnp.int32, (n_slots, n_experts), 0)
    wanted = jnp.where(slot < counts_ref[...], picks_ref[...], -1)
    positions = lax.broadcasted_iota(jnp.int32, (n_slots, n_tokens), 1)
    for e in range(n_experts):
        hit = wanted[:, e : e + 1] == positions
        sel_ref[e * n_slots : (e + 1) * n_slots, :] = hit.astype(jnp.float32).astype(
            jnp.bfloat16
        )
    both = jnp.concatenate([tokens_ref[...], cotangent_ref[...]], axis=1)
    picked = dot32(sel_ref[...], both).astype(jnp.bfloat16)
    for h in range(HI):
        out_ref[h] = picked


def expert_kernel(
    full_hbm,
    down_hbm,
    pre_hbm,
    gate_hbm,
    up_hbm,
    pre_grad_ref,
    parts_hbm,
    y,
    down,
    pre,
    gate,
    up,
    parts,
    y_sem,
    down_sem,
    up_sem,
    out_sem,
    pre_sem,
    gate_sem,
):
    n_rows, n_hi, capacity, _ = full_hbm.shape
    n_blocks, _, width = parts_hbm.shape
    units = pre.shape[1]
    per = n_blocks // CHUNKS
    span = per * width
    y_copies, down_copies, up_copies = [], [], []
    for c in range(CHUNKS):
        down_copies.append(
            pltpu.make_async_copy(
                down_hbm.at[:, pl.ds(c * span, span)],
                down.at[:, pl.ds(c * span, span)],
                down_sem.at[c],
            )
        )
        down_copies[-1].start()
        for b in range(c * per, (c + 1) * per):
            y_copies.append(
                pltpu.make_async_copy(
                    full_hbm.at[b % n_rows, b // n_rows, :, pl.ds(width, width)],
                    y.at[:, pl.ds(b * width, width)],
                    y_sem.at[b],
                )
            )
            y_copies[-1].start()
    pre_copy = pltpu.make_async_copy(pre_hbm, pre, pre_sem)
    gate_copy = pltpu.make_async_copy(gate_hbm, gate, gate_sem)
    pre_copy.start()
    gate_copy.start()
    for c in range(CHUNKS):
        up_copies.append(
            pltpu.make_async_copy(
                up_hbm.at[pl.ds(c * span, span)], up.at[pl.ds(c * span, span)], up_sem.at[c]
            )
        )
        up_copies[-1].start()
    back = jnp.zeros((capacity, units), jnp.float32)
    for c in range(CHUNKS):
        down_copies[c].wait()
        for b in range(c * per, (c + 1) * per):
            y_copies[b].wait()
        columns = slice(c * span, (c + 1) * span)
        back += dot32(y[:, columns], down[:, columns], NT)
    pre_copy.wait()
    gate_copy.wait()
    act = pre[...].astype(jnp.float32)
    pre_grad = jnp.where(act > 0, gate[...] * back, 0.0).astype(jnp.bfloat16)
    pre_grad_ref[...] = pre_grad
    row_sum = lax.dot_general(
        jnp.ones((8, units), jnp.float32),
        jnp.maximum(act, 0.0) * back,
        NT,
        precision=lax.Precision.HIGHEST,
        preferred_element_type=jnp.float32,
    )
    rows = lax.broadcasted_iota(jnp.int32, (8, width), 0)
    n_gate = capacity // width
    packed = jnp.zeros((8, width), jnp.float32)
    for k in range(n_gate):
        packed = jnp.where(
            rows % n_gate == k, row_sum[:, k * width : (k + 1) * width], packed
        )
    high = packed.astype(jnp.bfloat16).astype(jnp.float32)
    packed = jnp.where(rows < n_gate, high, packed - high)
    packed = jnp.concatenate([packed, jnp.zeros_like(packed)], axis=0).astype(
        jnp.bfloat16
    )
    out_copies = []
    for c in range(CHUNKS):
        up_copies[c].wait()
        part = dot32(pre_grad, up[c * span : (c + 1) * span, :], NT).astype(jnp.bfloat16)
        for b in range(per):
            parts[c * per + b, :capacity, :] = part[:, b * width : (b + 1) * width]
            parts[c * per + b, capacity:, :] = packed
        out_copies.append(
            pltpu.make_async_copy(
                parts.at[pl.ds(c * per, per)], parts_hbm.at[pl.ds(c * per, per)], out_sem.at[c]
            )
        )
        out_copies[-1].start()
    for copy in out_copies:
        copy.wait()


def down_kernel(y0_ref, y1_ref, pre_ref, gate_ref, out_ref, hidden_t):
    @pl.when(pl.program_id(0) == 0)
    def _():
        hidden_t[...] = (
            jnp.maximum(pre_ref[...].astype(jnp.float32), 0.0).T.astype(jnp.bfloat16)
        )

    pair = jnp.concatenate([y0_ref[0, 0], y1_ref[0, 0]], axis=1)
    scaled = (gate_ref[...] * pair.astype(jnp.float32)).astype(jnp.bfloat16)
    out_ref[...] = dot32(hidden_t[...], scaled).astype(jnp.bfloat16)


def up_kernel(x0_ref, x1_ref, pre_grad_ref, out_ref):
    pair = jnp.concatenate([x0_ref[0, 0], x1_ref[0, 0]], axis=1)
    out_ref[...] = dot32(pair, pre_grad_ref[...], TN).astype(jnp.bfloat16)


def combine_kernel(sel_ref, returned_ref, out_ref):
    out_ref[...] = dot32(sel_ref[...], returned_ref[...], TN).astype(jnp.bfloat16)


def cost(flops, nbytes):
    return pl.CostEstimate(flops=flops, bytes_accessed=nbytes, transcendentals=0)


def per_device(tokens, cotangent, w_up, w_down, saved_pre, gates, picks, counts):
    bf16 = jnp.bfloat16
    n_tokens, width = tokens.shape
    _, n_experts, n_slots = picks.shape
    _, d_model, units = w_up.shape
    capacity = n_experts * n_slots
    n_blocks = d_model // width
    n_rows = n_blocks // HI
    n_pairs = n_blocks // 2
    macs = capacity * units * d_model
    params = pltpu.CompilerParams(vmem_limit_bytes=VMEM_LIMIT)
    shape = jax.ShapeDtypeStruct
    whole = lambda *dims: pl.BlockSpec(dims, lambda i, *_: (0,) * len(dims))
    hbm = pl.BlockSpec(memory_space=pl.ANY)
    vmem = pl.BlockSpec(memory_space=pltpu.VMEM)

    selector, picked = pl.pallas_call(
        pick_kernel,
        out_shape=(
            shape((capacity, n_tokens), bf16),
            shape((HI, capacity, 2 * width), bf16),
        ),
    )(picks[0].T, counts, tokens, cotangent)
    arrived = lax.all_to_all(
        picked.reshape(HI * n_experts, n_slots, 2 * width), ("hi", "ep"), 0, 0, tiled=True
    ).reshape(HI, capacity, 2 * width)
    full = lax.all_gather(arrived, "row", axis=0, tiled=False)

    gate_column = gates[0][:, None]
    pre_grad, parts = pl.pallas_call(
        expert_kernel,
        in_specs=[hbm] * 5,
        out_specs=[vmem, hbm],
        out_shape=(
            shape((capacity, units), bf16),
            shape((n_blocks, capacity + EXTRA, width), bf16),
        ),
        scratch_shapes=[
            pltpu.VMEM((capacity, d_model), bf16),
            pltpu.VMEM((units, d_model), bf16),
            pltpu.VMEM((capacity, units), bf16),
            pltpu.VMEM((capacity, 1), jnp.float32),
            pltpu.VMEM((d_model, units), bf16),
            pltpu.VMEM((n_blocks, capacity + EXTRA, width), bf16),
            pltpu.SemaphoreType.DMA((n_blocks,)),
            pltpu.SemaphoreType.DMA((CHUNKS,)),
            pltpu.SemaphoreType.DMA((CHUNKS,)),
            pltpu.SemaphoreType.DMA((CHUNKS,)),
            pltpu.SemaphoreType.DMA,
            pltpu.SemaphoreType.DMA,
        ],
        compiler_params=params,
        cost_estimate=cost(4 * macs, 7 << 20),
    )(full, w_down[0], saved_pre[0], gate_column, w_up[0])
    swapped = lax.all_to_all(parts, ("hi", "row"), 0, 0, tiled=True)

    def block(which, odd):
        def place(i):
            first = 2 * i + odd
            return first % n_rows, first // n_rows, 0, which
        return pl.BlockSpec((1, 1, capacity, width), place)

    grad_down = pl.pallas_call(
        down_kernel,
        grid=(n_pairs,),
        in_specs=[block(1, 0), block(1, 1), whole(capacity, units), whole(capacity, 1)],
        out_specs=pl.BlockSpec((units, 2 * width), lambda i: (0, i)),
        out_shape=shape((units, d_model), bf16),
        scratch_shapes=[pltpu.VMEM((units, capacity), bf16)],
        compiler_params=params,
        cost_estimate=cost(2 * macs, 4 << 20),
    )(full, full, saved_pre[0], gate_column)
    grad_up = pl.pallas_call(
        up_kernel,
        grid=(n_pairs,),
        in_specs=[block(0, 0), block(0, 1), whole(capacity, units)],
        out_specs=pl.BlockSpec((2 * width, units), lambda i: (i, 0)),
        out_shape=shape((d_model, units), bf16),
        compiler_params=params,
        cost_estimate=cost(2 * macs, 4 << 20),
    )(full, full, pre_grad)

    swapped, grad_down, grad_up = lax.optimization_barrier((swapped, grad_down, grad_up))
    summed = jnp.sum(swapped[:, :capacity].astype(jnp.float32), axis=0).astype(bf16)
    n_gate = capacity // width
    gate_rows = jnp.sum(swapped[:, capacity:].astype(jnp.float32), axis=0)
    gate_total = (gate_rows[:n_gate] + gate_rows[n_gate : 2 * n_gate]).reshape(1, capacity)
    returned = lax.all_to_all(
        summed.reshape(n_experts, n_slots, width), "ep", 0, 0, tiled=True
    ).reshape(capacity, width)
    grad_tokens = pl.pallas_call(
        combine_kernel, out_shape=shape((n_tokens, width), bf16)
    )(selector, returned)
    return grad_tokens, grad_up[None], grad_down[None], gate_total


def solution(mesh):
    n_ep, n_et = mesh.devices.shape
    fine = Mesh(mesh.devices.reshape(n_ep, HI, n_et // HI), ("ep", "hi", "row"))
    et = ("hi", "row")
    in_specs = (
        P("ep", et),
        P("ep", et),
        P("ep", None, et),
        P("ep", et, None),
        P("ep", None, et),
        P("ep", None),
        P("ep", None, None),
        P("ep", None),
    )
    out_specs = (P("ep", et), P("ep", None, et), P("ep", et, None), P("ep", None))
    return jax.shard_map(
        per_device, mesh=fine, in_specs=in_specs, out_specs=out_specs, check_vma=False
    )
```

```python
import functools

import jax
import jax.numpy as jnp
from jax import lax
from jax.experimental import pallas as pl
from jax.experimental.pallas import tpu as pltpu
from jax.sharding import Mesh, PartitionSpec as P

HI = 2
EXTRA = 16
NN = (((1,), (0,)), ((), ()))
NT = (((1,), (1,)), ((), ()))
TN = (((0,), (0,)), ((), ()))
VMEM_LIMIT = 20 << 20


def dot32(a, b, dims=NN):
    return lax.dot_general(a, b, dims, preferred_element_type=jnp.float32)


def pick_kernel(picks_ref, counts_ref, tokens_ref, cotangent_ref, sel_ref, out_ref):
    n_slots, n_experts = picks_ref.shape
    n_tokens = tokens_ref.shape[0]
    slot = lax.broadcasted_iota(jnp.int32, (n_slots, n_experts), 0)
    wanted = jnp.where(slot < counts_ref[...], picks_ref[...], -1)
    positions = lax.broadcasted_iota(jnp.int32, (n_slots, n_tokens), 1)
    for e in range(n_experts):
        hit = wanted[:, e : e + 1] == positions
        sel_ref[e * n_slots : (e + 1) * n_slots, :] = hit.astype(jnp.float32).astype(
            jnp.bfloat16
        )
    both = jnp.concatenate([tokens_ref[...], cotangent_ref[...]], axis=1)
    picked = dot32(sel_ref[...], both).astype(jnp.bfloat16)
    for h in range(HI):
        out_ref[h] = picked


def place(order_ref, h, d):
    n_rows = order_ref.shape[0] // HI
    return pl.multiple_of(order_ref[h * n_rows + d % n_rows] * 128, 128)


def half_of(blocks, n, h, side):
    width = blocks[0].shape[-1] // 2
    if len(blocks) == 1:
        return blocks[0][h, :, side * width : (side + 1) * width]
    return blocks[h][0, :, side * width : (side + 1) * width]


def grouped(refs, distances, n_rows):
    groups, at = [], 0
    for d in distances:
        count = 2 if d == n_rows // 2 else 1
        groups.append(refs[at : at + count])
        at += count
    return groups, refs[at:]


def load_columns(order_ref, source, target, sems, distances, axis):
    copies = []
    for k, d in enumerate(distances):
        for h in range(HI):
            at = pl.ds(place(order_ref, h, d), 128)
            to = pl.ds((k * HI + h) * 128, 128)
            copies.append(
                pltpu.make_async_copy(
                    source.at[:, at] if axis else source.at[at],
                    target.at[:, to] if axis else target.at[to],
                    sems.at[k * HI + h],
                )
            )
            copies[-1].start()
    return copies


def back_kernel(distances, n_rows, last, order_ref, *refs):
    groups, rest = grouped(refs, distances, n_rows)
    if last:
        down_hbm, before_ref, pre_ref, gate_ref, pre_grad_ref, gate_out, down, sems = rest
    else:
        down_hbm, back_ref, down, sems = rest
    copies = load_columns(order_ref, down_hbm, down, sems, distances, 1)
    back = before_ref[...] if last else None
    for k in range(len(distances)):
        for h in range(HI):
            copies[k * HI + h].wait()
        pair = jnp.concatenate(
            [half_of(groups[k], n_rows, h, 1) for h in range(HI)], axis=1
        )
        term = dot32(pair, down[:, k * HI * 128 : (k + 1) * HI * 128], NT)
        back = term if back is None else back + term
    if not last:
        back_ref[...] = back
        return
    act = pre_ref[...].astype(jnp.float32)
    pre_grad_ref[...] = jnp.where(act > 0, gate_ref[...] * back, 0.0).astype(jnp.bfloat16)
    capacity, units = act.shape
    row_sum = lax.dot_general(
        jnp.ones((8, units), jnp.float32),
        jnp.maximum(act, 0.0) * back,
        NT,
        precision=lax.Precision.HIGHEST,
        preferred_element_type=jnp.float32,
    )
    rows = lax.broadcasted_iota(jnp.int32, (8, 128), 0)
    n_gate = capacity // 128
    packed = jnp.zeros((8, 128), jnp.float32)
    for k in range(n_gate):
        packed = jnp.where(
            rows % n_gate == k, row_sum[:, k * 128 : (k + 1) * 128], packed
        )
    high = packed.astype(jnp.bfloat16).astype(jnp.float32)
    packed = jnp.where(rows < n_gate, high, packed - high)
    gate_out[...] = jnp.concatenate([packed, jnp.zeros_like(packed)], axis=0)


def own_parts(order_ref, pre_grad_ref, up_hbm, up, sems, wanted):
    copies = []
    for k, (d, h) in enumerate(wanted):
        copies.append(
            pltpu.make_async_copy(
                up_hbm.at[pl.ds(place(order_ref, h, d), 128)],
                up.at[pl.ds(k * 128, 128)],
                sems.at[k],
            )
        )
        copies[-1].start()
    for copy in copies:
        copy.wait()
    parts = dot32(pre_grad_ref[...], up[...], NT)
    return [parts[:, k * 128 : (k + 1) * 128] for k in range(len(wanted))]


def first_kernel(d, h, order_ref, pre_grad_ref, gate_ref, up_hbm, out_ref, up, sems):
    (part,) = own_parts(order_ref, pre_grad_ref, up_hbm, up, sems, [(d, h)])
    capacity = pre_grad_ref.shape[0]
    out_ref[0, :capacity, :] = part.astype(jnp.bfloat16)
    out_ref[0, capacity:, :] = gate_ref[...].astype(jnp.bfloat16)


def pass_kernel(
    d, only, order_ref, came, pre_grad_ref, total_ref, up_hbm, out_ref, total_out, up, sems
):
    parts = own_parts(order_ref, pre_grad_ref, up_hbm, up, sems, [(d, 0), (d, 1)])
    capacity = pre_grad_ref.shape[0]
    for h in range(HI):
        part = parts[h]
        if only is None:
            part = part + came[h, :capacity, :].astype(jnp.float32)
        elif h == only:
            part = part + came[0, :capacity, :].astype(jnp.float32)
        out_ref[h, :capacity, :] = part.astype(jnp.bfloat16)
        out_ref[h, capacity:, :] = came[0, capacity:, :]
    total_out[...] = total_ref[...] + came[0, capacity:, :].astype(jnp.float32)


def last_kernel(
    order_ref, from_left, from_right, pre_grad_ref, total_left, total_right, up_hbm,
    sum_ref, gate_out, up, sems,
):
    parts = own_parts(order_ref, pre_grad_ref, up_hbm, up, sems, [(0, 0), (0, 1)])
    capacity = pre_grad_ref.shape[0]
    for h in range(HI):
        sum_ref[h] = (
            parts[h]
            + from_left[h, :capacity, :].astype(jnp.float32)
            + from_right[h, :capacity, :].astype(jnp.float32)
        ).astype(jnp.bfloat16)
    n_gate = capacity // 128
    total = total_left[...] + total_right[...] + from_left[0, capacity:, :].astype(jnp.float32)
    gate_out[...] = total[:n_gate] + total[n_gate : 2 * n_gate]


def down_kernel(distances, n_rows, more, order_ref, *refs):
    groups, rest = grouped(refs, distances, n_rows)
    if more:
        pre_ref, gate_ref, _, out_hbm, out, sems = rest
    else:
        pre_ref, gate_ref, out_hbm, out, sems = rest
    hidden_t = jnp.maximum(pre_ref[...].astype(jnp.float32), 0.0).T.astype(jnp.bfloat16)
    copies = []
    for k, d in enumerate(distances):
        pair = jnp.concatenate(
            [half_of(groups[k], n_rows, h, 1) for h in range(HI)], axis=1
        )
        scaled = (gate_ref[...] * pair.astype(jnp.float32)).astype(jnp.bfloat16)
        out[:, k * HI * 128 : (k + 1) * HI * 128] = dot32(hidden_t, scaled).astype(
            jnp.bfloat16
        )
        for h in range(HI):
            copies.append(
                pltpu.make_async_copy(
                    out.at[:, pl.ds((k * HI + h) * 128, 128)],
                    out_hbm.at[:, pl.ds(place(order_ref, h, d), 128)],
                    sems.at[k * HI + h],
                )
            )
            copies[-1].start()
    for copy in copies:
        copy.wait()


def up_kernel(distances, n_rows, more, order_ref, *refs):
    groups, rest = grouped(refs, distances, n_rows)
    if more:
        pre_grad_ref, _, out_hbm, out, sems = rest
    else:
        pre_grad_ref, out_hbm, out, sems = rest
    copies = []
    for k, d in enumerate(distances):
        pair = jnp.concatenate(
            [half_of(groups[k], n_rows, h, 0) for h in range(HI)], axis=1
        )
        out[k * HI * 128 : (k + 1) * HI * 128, :] = dot32(
            pair, pre_grad_ref[...], TN
        ).astype(jnp.bfloat16)
        for h in range(HI):
            copies.append(
                pltpu.make_async_copy(
                    out.at[pl.ds((k * HI + h) * 128, 128)],
                    out_hbm.at[pl.ds(place(order_ref, h, d), 128)],
                    sems.at[k * HI + h],
                )
            )
            copies[-1].start()
    for copy in copies:
        copy.wait()


def combine_kernel(sel_ref, returned_ref, out_ref):
    both = jnp.concatenate([returned_ref[h] for h in range(HI)], axis=1)
    total = dot32(sel_ref[...], both, TN)
    width = out_ref.shape[1]
    out_ref[...] = (total[:, :width] + total[:, width:]).astype(jnp.bfloat16)


def cost(flops, nbytes):
    return pl.CostEstimate(flops=flops, bytes_accessed=nbytes, transcendentals=0)


def per_device(tokens, cotangent, w_up, w_down, saved_pre, gates, picks, counts):
    bf16, f32 = jnp.bfloat16, jnp.float32
    n_tokens, width = tokens.shape
    _, n_experts, n_slots = picks.shape
    _, d_model, units = w_up.shape
    capacity = n_experts * n_slots
    n_rows = d_model // width // HI
    far = n_rows // 2
    macs = capacity * units * width * HI
    params = pltpu.CompilerParams(vmem_limit_bytes=VMEM_LIMIT)
    shape = jax.ShapeDtypeStruct
    hbm = pl.BlockSpec(memory_space=pl.ANY)
    vmem = pl.BlockSpec(memory_space=pltpu.VMEM)
    smem = pl.BlockSpec(memory_space=pltpu.SMEM)
    dma = pltpu.SemaphoreType.DMA

    def right(a):
        return lax.ppermute(a, "row", [(i, (i + 1) % n_rows) for i in range(n_rows)])

    def left(a):
        return lax.ppermute(a, "row", [(i, (i - 1) % n_rows) for i in range(n_rows)])

    hi, row = lax.axis_index("hi"), lax.axis_index("row")
    ahead_of = (row + jnp.arange(n_rows, dtype=jnp.int32)) % n_rows
    order = jnp.concatenate([h * n_rows + ahead_of for h in range(HI)])
    del hi
    gate_column = gates[0][:, None]
    pre, w_first, w_second = saved_pre[0], w_up[0], w_down[0]

    selector, picked = pl.pallas_call(
        pick_kernel,
        out_shape=(
            shape((capacity, n_tokens), bf16),
            shape((HI, capacity, 2 * width), bf16),
        ),
    )(picks[0].T, counts, tokens, cotangent)
    arrived = lax.all_to_all(
        picked.reshape(HI * n_experts, n_slots, 2 * width), ("hi", "ep"), 0, 0, tiled=True
    ).reshape(HI, capacity, 2 * width)

    blocks = {0: [arrived]}
    behind = ahead = arrived
    for d in range(1, far):
        behind, ahead = right(behind), left(ahead)
        blocks[-d], blocks[d] = [behind], [ahead]
    late = [far - 1, 1 - far, far]
    early = [d for d in blocks if d not in late]
    flat = lambda distances: [b for d in distances for b in blocks[d]]
    columns = lambda n: [pltpu.VMEM((units, n * HI * width), bf16), dma((n * HI,))]
    rows_of = lambda n: [pltpu.VMEM((n * width, units), bf16), dma((n,))]

    back = pl.pallas_call(
        functools.partial(back_kernel, early, n_rows, False),
        in_specs=[smem] + [vmem] * len(flat(early)) + [hbm],
        out_specs=vmem,
        out_shape=shape((capacity, units), f32),
        scratch_shapes=columns(len(early)),
        compiler_params=params,
        cost_estimate=cost(2 * macs * len(early), 4 << 20),
    )(order, *flat(early), w_second)
    down_early = pl.pallas_call(
        functools.partial(down_kernel, early, n_rows, False),
        in_specs=[smem] + [vmem] * (len(flat(early)) + 2),
        out_specs=hbm,
        out_shape=shape((units, d_model), bf16),
        scratch_shapes=columns(len(early)),
        compiler_params=params,
        cost_estimate=cost(2 * macs * len(early), 4 << 20),
    )(order, *flat(early), pre, gate_column)
    behind, ahead, back, down_early = lax.optimization_barrier(
        (behind, ahead, back, down_early)
    )
    blocks[1 - far], blocks[far - 1] = [behind], [ahead]
    blocks[far] = [right(behind[:1]), left(ahead[1:])]
    pre_grad, gate_mine = pl.pallas_call(
        functools.partial(back_kernel, late, n_rows, True),
        in_specs=[smem] + [vmem] * len(flat(late)) + [hbm, vmem, vmem, vmem],
        out_specs=[vmem, vmem],
        out_shape=(shape((capacity, units), bf16), shape((EXTRA, width), f32)),
        scratch_shapes=columns(len(late)),
        compiler_params=params,
        cost_estimate=cost(2 * macs * len(late), 3 << 20),
    )(order, *flat(late), w_second, back, pre, gate_column)

    grad_down = pl.pallas_call(
        functools.partial(down_kernel, late, n_rows, True),
        in_specs=[smem] + [vmem] * (len(flat(late)) + 2) + [hbm],
        out_specs=hbm,
        out_shape=shape((units, d_model), bf16),
        input_output_aliases={len(flat(late)) + 3: 0},
        scratch_shapes=columns(len(late)),
        compiler_params=params,
        cost_estimate=cost(2 * macs * len(late), 3 << 20),
    )(order, *flat(late), pre, gate_column, down_early)
    up_call = functools.partial(
        pl.pallas_call,
        out_specs=hbm,
        out_shape=shape((d_model, units), bf16),
        compiler_params=params,
        cost_estimate=cost(2 * macs * 4, 4 << 20),
    )
    up_early = up_call(
        functools.partial(up_kernel, early, n_rows, False),
        in_specs=[smem] + [vmem] * (len(flat(early)) + 1),
        scratch_shapes=rows_of(len(early) * HI),
    )(order, *flat(early), pre_grad)
    message = lambda n: shape((n, capacity + EXTRA, width), bf16)
    def begin(d, h):
        return pl.pallas_call(
            functools.partial(first_kernel, d, h),
            in_specs=[smem, vmem, vmem, hbm],
            out_specs=vmem,
            out_shape=message(1),
            scratch_shapes=rows_of(1),
            compiler_params=params,
            cost_estimate=cost(macs, 1 << 20),
        )(order, pre_grad, gate_mine, w_first)

    def carry_on(d, only, came, total):
        return pl.pallas_call(
            functools.partial(pass_kernel, d, only),
            in_specs=[smem, vmem, vmem, vmem, hbm],
            out_specs=[vmem, vmem],
            out_shape=(message(HI), shape((EXTRA, width), f32)),
            scratch_shapes=rows_of(HI),
            compiler_params=params,
            cost_estimate=cost(2 * macs, 1 << 20),
        )(order, came, pre_grad, total, w_first)

    from_left, from_right = right(begin(far, 0)), left(begin(far, 1))
    total_left, total_right = gate_mine, jnp.zeros_like(gate_mine)
    for d in range(far - 1, 0, -1):
        start = d == far - 1
        if d == 1:
            from_left, grad_down = lax.optimization_barrier((from_left, grad_down))
        go_right, total_left = carry_on(d, 0 if start else None, from_left, total_left)
        go_left, total_right = carry_on(-d, 1 if start else None, from_right, total_right)
        from_left, from_right = right(go_right), left(go_left)
    from_left, up_early = lax.optimization_barrier((from_left, up_early))
    grad_up = up_call(
        functools.partial(up_kernel, late, n_rows, True),
        in_specs=[smem] + [vmem] * (len(flat(late)) + 1) + [hbm],
        input_output_aliases={len(flat(late)) + 2: 0},
        scratch_shapes=rows_of(len(late) * HI),
    )(order, *flat(late), pre_grad, up_early)
    n_gate = capacity // width
    summed, gate_half = pl.pallas_call(
        last_kernel,
        in_specs=[smem, vmem, vmem, vmem, vmem, vmem, hbm],
        out_specs=[vmem, vmem],
        out_shape=(shape((HI, capacity, width), bf16), shape((n_gate, width), f32)),
        scratch_shapes=rows_of(HI),
        compiler_params=params,
        cost_estimate=cost(2 * macs, 2 << 20),
    )(order, from_left, from_right, pre_grad, total_left, total_right, w_first)
    gate_total = gate_half + lax.ppermute(gate_half, "hi", [(0, 1), (1, 0)])
    returned = lax.all_to_all(
        summed.reshape(HI * n_experts, n_slots, width), ("hi", "ep"), 0, 0, tiled=True
    ).reshape(HI, capacity, width)

    grad_tokens = pl.pallas_call(
        combine_kernel,
        out_shape=shape((n_tokens, width), bf16),
        compiler_params=params,
    )(selector, returned)
    return grad_tokens, grad_up[None], grad_down[None], gate_total.reshape(1, capacity)


def solution(mesh):
    n_ep, n_et = mesh.devices.shape
    fine = Mesh(mesh.devices.reshape(n_ep, HI, n_et // HI), ("ep", "hi", "row"))
    et = ("hi", "row")
    in_specs = (
        P("ep", et),
        P("ep", et),
        P("ep", None, et),
        P("ep", et, None),
        P("ep", None, et),
        P("ep", None),
        P("ep", None, None),
        P("ep", None),
    )
    out_specs = (P("ep", et), P("ep", None, et), P("ep", et, None), P("ep", None))
    return jax.shard_map(
        per_device, mesh=fine, in_specs=in_specs, out_specs=out_specs, check_vma=False
    )
```

```python
import functools

import jax
import jax.numpy as jnp
from jax import lax
from jax.experimental import pallas as pl
from jax.experimental.pallas import tpu as pltpu
from jax.sharding import Mesh, PartitionSpec as P

HI = 2
EXTRA = 16
NN = (((1,), (0,)), ((), ()))
NT = (((1,), (1,)), ((), ()))
TN = (((0,), (0,)), ((), ()))
VMEM_LIMIT = 12 << 20


def dot32(a, b, dims=NN):
    return lax.dot_general(a, b, dims, preferred_element_type=jnp.float32)


def pick_kernel(picks_ref, counts_ref, tokens_ref, cotangent_ref, sel_ref, out_ref):
    n_slots, n_experts = picks_ref.shape
    n_tokens = tokens_ref.shape[0]
    slot = lax.broadcasted_iota(jnp.int32, (n_slots, n_experts), 0)
    wanted = jnp.where(slot < counts_ref[...], picks_ref[...], -1)
    positions = lax.broadcasted_iota(jnp.int32, (n_slots, n_tokens), 1)
    for e in range(n_experts):
        hit = wanted[:, e : e + 1] == positions
        sel_ref[e * n_slots : (e + 1) * n_slots, :] = hit.astype(jnp.float32).astype(
            jnp.bfloat16
        )
    both = jnp.concatenate([tokens_ref[...], cotangent_ref[...]], axis=1)
    picked = dot32(sel_ref[...], both).astype(jnp.bfloat16)
    for h in range(HI):
        out_ref[h] = picked


def place(order_ref, h, d):
    n_rows = order_ref.shape[0] // HI
    return pl.multiple_of(order_ref[h * n_rows + d % n_rows] * 128, 128)


def y_of(blocks, h):
    return blocks[0][2 * h] if len(blocks) == 1 else blocks[h][0]


def pack_kernel(hi_ref, arrived_ref, out_ref):
    width = out_ref.shape[-1]
    out_ref[0] = arrived_ref[0, :, width:]
    out_ref[1] = arrived_ref[hi_ref[0], :, :width]
    out_ref[2] = arrived_ref[1, :, width:]


def stack_kernel(*refs):
    for k, ref in enumerate(refs[:-1]):
        refs[-1][k] = ref[0]


def grouped(refs, distances, n_rows):
    groups, at = [], 0
    for d in distances:
        count = 2 if d == n_rows // 2 else 1
        groups.append(refs[at : at + count])
        at += count
    return groups, refs[at:]


def load_columns(order_ref, source, target, sems, distances, axis):
    copies = []
    for k, d in enumerate(distances):
        for h in range(HI):
            at = pl.ds(place(order_ref, h, d), 128)
            to = pl.ds((k * HI + h) * 128, 128)
            copies.append(
                pltpu.make_async_copy(
                    source.at[:, at] if axis else source.at[at],
                    target.at[:, to] if axis else target.at[to],
                    sems.at[k * HI + h],
                )
            )
            copies[-1].start()
    return copies


def back_kernel(distances, n_rows, last, order_ref, *refs):
    groups, rest = grouped(refs, distances, n_rows)
    if last:
        down_hbm, before_ref, pre_ref, gate_ref, pre_grad_ref, gate_out, down, sems = rest
    else:
        down_hbm, back_ref, down, sems = rest
    copies = load_columns(order_ref, down_hbm, down, sems, distances, 1)
    back = before_ref[...] if last else None
    for k in range(len(distances)):
        for h in range(HI):
            copies[k * HI + h].wait()
        pair = jnp.concatenate(
            [y_of(groups[k], h) for h in range(HI)], axis=1
        )
        term = dot32(pair, down[:, k * HI * 128 : (k + 1) * HI * 128], NT)
        back = term if back is None else back + term
    if not last:
        back_ref[...] = back
        return
    act = pre_ref[...].astype(jnp.float32)
    pre_grad_ref[...] = jnp.where(act > 0, gate_ref[...] * back, 0.0).astype(jnp.bfloat16)
    capacity, units = act.shape
    row_sum = lax.dot_general(
        jnp.ones((8, units), jnp.float32),
        jnp.maximum(act, 0.0) * back,
        NT,
        precision=lax.Precision.HIGHEST,
        preferred_element_type=jnp.float32,
    )
    rows = lax.broadcasted_iota(jnp.int32, (8, 128), 0)
    n_gate = capacity // 128
    packed = jnp.zeros((8, 128), jnp.float32)
    for k in range(n_gate):
        packed = jnp.where(
            rows % n_gate == k, row_sum[:, k * 128 : (k + 1) * 128], packed
        )
    high = packed.astype(jnp.bfloat16).astype(jnp.float32)
    packed = jnp.where(rows < n_gate, high, packed - high)
    gate_out[...] = jnp.concatenate([packed, jnp.zeros_like(packed)], axis=0)


def own_parts(order_ref, pre_grad_ref, up_hbm, up, sems, wanted):
    copies = []
    for k, (d, h) in enumerate(wanted):
        copies.append(
            pltpu.make_async_copy(
                up_hbm.at[pl.ds(place(order_ref, h, d), 128)],
                up.at[pl.ds(k * 128, 128)],
                sems.at[k],
            )
        )
        copies[-1].start()
    for copy in copies:
        copy.wait()
    parts = dot32(pre_grad_ref[...], up[...], NT)
    return [parts[:, k * 128 : (k + 1) * 128] for k in range(len(wanted))]


def first_kernel(d, h, order_ref, pre_grad_ref, gate_ref, up_hbm, out_ref, up, sems):
    (part,) = own_parts(order_ref, pre_grad_ref, up_hbm, up, sems, [(d, h)])
    capacity = pre_grad_ref.shape[0]
    out_ref[0, :capacity, :] = part.astype(jnp.bfloat16)
    out_ref[0, capacity:, :] = gate_ref[...].astype(jnp.bfloat16)


def pass_kernel(
    d, only, order_ref, came, pre_grad_ref, total_ref, up_hbm, out_ref, total_out, up, sems
):
    parts = own_parts(order_ref, pre_grad_ref, up_hbm, up, sems, [(d, 0), (d, 1)])
    capacity = pre_grad_ref.shape[0]
    for h in range(HI):
        part = parts[h]
        if only is None:
            part = part + came[h, :capacity, :].astype(jnp.float32)
        elif h == only:
            part = part + came[0, :capacity, :].astype(jnp.float32)
        out_ref[h, :capacity, :] = part.astype(jnp.bfloat16)
        out_ref[h, capacity:, :] = came[0, capacity:, :]
    total_out[...] = total_ref[...] + came[0, capacity:, :].astype(jnp.float32)


def last_kernel(
    order_ref, from_left, from_right, pre_grad_ref, total_left, total_right, up_hbm,
    sum_ref, gate_out, up, sems,
):
    parts = own_parts(order_ref, pre_grad_ref, up_hbm, up, sems, [(0, 0), (0, 1)])
    capacity = pre_grad_ref.shape[0]
    for h in range(HI):
        sum_ref[h] = (
            parts[h]
            + from_left[h, :capacity, :].astype(jnp.float32)
            + from_right[h, :capacity, :].astype(jnp.float32)
        ).astype(jnp.bfloat16)
    n_gate = capacity // 128
    total = total_left[...] + total_right[...] + from_left[0, capacity:, :].astype(jnp.float32)
    gate_out[...] = total[:n_gate] + total[n_gate : 2 * n_gate]


def down_kernel(distances, n_rows, more, order_ref, *refs):
    groups, rest = grouped(refs, distances, n_rows)
    if more:
        pre_ref, gate_ref, _, out_hbm, out, sems = rest
    else:
        pre_ref, gate_ref, out_hbm, out, sems = rest
    hidden_t = jnp.maximum(pre_ref[...].astype(jnp.float32), 0.0).T.astype(jnp.bfloat16)
    copies = []
    for k, d in enumerate(distances):
        pair = jnp.concatenate(
            [y_of(groups[k], h) for h in range(HI)], axis=1
        )
        scaled = (gate_ref[...] * pair.astype(jnp.float32)).astype(jnp.bfloat16)
        out[:, k * HI * 128 : (k + 1) * HI * 128] = dot32(hidden_t, scaled).astype(
            jnp.bfloat16
        )
        for h in range(HI):
            copies.append(
                pltpu.make_async_copy(
                    out.at[:, pl.ds((k * HI + h) * 128, 128)],
                    out_hbm.at[:, pl.ds(place(order_ref, h, d), 128)],
                    sems.at[k * HI + h],
                )
            )
            copies[-1].start()
    for copy in copies:
        copy.wait()


def up_kernel(distances, more, order_ref, own_ref, other_ref, pre_grad_ref, *refs):
    out_hbm, out, sems = refs[1:] if more else refs
    copies = []
    for k, d in enumerate(distances):
        pair = jnp.concatenate([own_ref[k], other_ref[k]], axis=1)
        out[k * HI * 128 : (k + 1) * HI * 128, :] = dot32(
            pair, pre_grad_ref[...], TN
        ).astype(jnp.bfloat16)
        for h in range(HI):
            copies.append(
                pltpu.make_async_copy(
                    out.at[pl.ds((k * HI + h) * 128, 128)],
                    out_hbm.at[pl.ds(place(order_ref, h, d), 128)],
                    sems.at[k * HI + h],
                )
            )
            copies[-1].start()
    for copy in copies:
        copy.wait()


def combine_kernel(sel_ref, returned_ref, out_ref):
    both = jnp.concatenate([returned_ref[h] for h in range(HI)], axis=1)
    total = dot32(sel_ref[...], both, TN)
    width = out_ref.shape[1]
    out_ref[...] = (total[:, :width] + total[:, width:]).astype(jnp.bfloat16)


def cost(flops, nbytes):
    return pl.CostEstimate(flops=flops, bytes_accessed=nbytes, transcendentals=0)


def per_device(tokens, cotangent, w_up, w_down, saved_pre, gates, picks, counts):
    bf16, f32 = jnp.bfloat16, jnp.float32
    n_tokens, width = tokens.shape
    _, n_experts, n_slots = picks.shape
    _, d_model, units = w_up.shape
    capacity = n_experts * n_slots
    n_rows = d_model // width // HI
    far = n_rows // 2
    macs = capacity * units * width * HI
    params = pltpu.CompilerParams(vmem_limit_bytes=VMEM_LIMIT)
    shape = jax.ShapeDtypeStruct
    hbm = pl.BlockSpec(memory_space=pl.ANY)
    vmem = pl.BlockSpec(memory_space=pltpu.VMEM)
    smem = pl.BlockSpec(memory_space=pltpu.SMEM)
    dma = pltpu.SemaphoreType.DMA

    def right(a):
        return lax.ppermute(a, "row", [(i, (i + 1) % n_rows) for i in range(n_rows)])

    def left(a):
        return lax.ppermute(a, "row", [(i, (i - 1) % n_rows) for i in range(n_rows)])

    hi, row = lax.axis_index("hi"), lax.axis_index("row")
    ahead_of = (row + jnp.arange(n_rows, dtype=jnp.int32)) % n_rows
    order = jnp.concatenate([h * n_rows + ahead_of for h in range(HI)])
    order_x = jnp.concatenate([h * n_rows + ahead_of for h in (hi, 1 - hi)])
    gate_column = gates[0][:, None]
    pre, w_first, w_second = saved_pre[0], w_up[0], w_down[0]

    selector, picked = pl.pallas_call(
        pick_kernel,
        out_shape=(
            shape((capacity, n_tokens), bf16),
            shape((HI, capacity, 2 * width), bf16),
        ),
    )(picks[0].T, counts, tokens, cotangent)
    arrived = lax.all_to_all(
        picked.reshape(HI * n_experts, n_slots, 2 * width), ("hi", "ep"), 0, 0, tiled=True
    ).reshape(HI, capacity, 2 * width)

    arrived, order, order_x, gate_column = lax.optimization_barrier(
        (arrived, order, order_x, gate_column)
    )
    packed = pl.pallas_call(
        pack_kernel,
        in_specs=[smem, vmem],
        out_specs=vmem,
        out_shape=shape((HI + 1, capacity, width), bf16),
        compiler_params=params,
    )(hi[None], arrived)

    def stacked(pieces):
        return pl.pallas_call(
            stack_kernel,
            grid=(1,),
            in_specs=[pl.BlockSpec((1, capacity, width), lambda i: (1, 0, 0))]
            * len(pieces),
            out_specs=pl.BlockSpec((len(pieces), capacity, width), lambda i: (0, 0, 0)),
            out_shape=shape((len(pieces), capacity, width), bf16),
            compiler_params=params,
            cost_estimate=cost(0, 2 << 20),
        )(*pieces)

    def crossed(a):
        return lax.ppermute(a, "hi", [(0, 1), (1, 0)])

    blocks = {0: [packed]}
    behind = ahead = packed
    near = (0, -1, 1)
    for d in range(1, far):
        behind, ahead = right(behind), left(ahead)
        blocks[-d], blocks[d] = [behind], [ahead]
        if d == 1:
            x_near = stacked([blocks[k][0] for k in near])
            x_near_other = crossed(x_near)
    late = [far - 1, 1 - far, far]
    early = [d for d in blocks if d not in late]
    flat = lambda distances: [b for d in distances for b in blocks[d]]
    columns = lambda n: [pltpu.VMEM((units, n * HI * width), bf16), dma((n * HI,))]
    rows_of = lambda n: [pltpu.VMEM((n * width, units), bf16), dma((n,))]

    back = pl.pallas_call(
        functools.partial(back_kernel, early, n_rows, False),
        in_specs=[smem] + [vmem] * len(flat(early)) + [hbm],
        out_specs=vmem,
        out_shape=shape((capacity, units), f32),
        scratch_shapes=columns(len(early)),
        compiler_params=params,
        cost_estimate=cost(2 * macs * len(early), 4 << 20),
    )(order, *flat(early), w_second)
    down_early = pl.pallas_call(
        functools.partial(down_kernel, early, n_rows, False),
        in_specs=[smem] + [vmem] * (len(flat(early)) + 2),
        out_specs=hbm,
        out_shape=shape((units, d_model), bf16),
        scratch_shapes=columns(len(early)),
        compiler_params=params,
        cost_estimate=cost(2 * macs * len(early), 4 << 20),
    )(order, *flat(early), pre, gate_column)
    behind, ahead, back, down_early, x_near_other = lax.optimization_barrier(
        (behind, ahead, back, down_early, x_near_other)
    )
    blocks[1 - far], blocks[far - 1] = [behind], [ahead]
    blocks[far] = [right(behind[:2]), left(ahead[2:])]
    rest = [d for d in blocks if d not in near]
    x_rest = stacked([blocks[d][0] for d in rest])
    x_rest_other = crossed(x_rest)
    pre_grad, gate_mine = pl.pallas_call(
        functools.partial(back_kernel, late, n_rows, True),
        in_specs=[smem] + [vmem] * len(flat(late)) + [hbm, vmem, vmem, vmem],
        out_specs=[vmem, vmem],
        out_shape=(shape((capacity, units), bf16), shape((EXTRA, width), f32)),
        scratch_shapes=columns(len(late)),
        compiler_params=params,
        cost_estimate=cost(2 * macs * len(late), 3 << 20),
    )(order, *flat(late), w_second, back, pre, gate_column)

    grad_down = pl.pallas_call(
        functools.partial(down_kernel, late, n_rows, True),
        in_specs=[smem] + [vmem] * (len(flat(late)) + 2) + [hbm],
        out_specs=hbm,
        out_shape=shape((units, d_model), bf16),
        input_output_aliases={len(flat(late)) + 3: 0},
        scratch_shapes=columns(len(late)),
        compiler_params=params,
        cost_estimate=cost(2 * macs * len(late), 3 << 20),
    )(order, *flat(late), pre, gate_column, down_early)
    up_call = functools.partial(
        pl.pallas_call,
        out_specs=hbm,
        out_shape=shape((d_model, units), bf16),
        compiler_params=params,
        cost_estimate=cost(2 * macs * 4, 4 << 20),
    )
    message = lambda n: shape((n, capacity + EXTRA, width), bf16)
    def begin(d, h):
        return pl.pallas_call(
            functools.partial(first_kernel, d, h),
            in_specs=[smem, vmem, vmem, hbm],
            out_specs=vmem,
            out_shape=message(1),
            scratch_shapes=rows_of(1),
            compiler_params=params,
            cost_estimate=cost(macs, 1 << 20),
        )(order, pre_grad, gate_mine, w_first)

    def carry_on(d, only, came, total):
        return pl.pallas_call(
            functools.partial(pass_kernel, d, only),
            in_specs=[smem, vmem, vmem, vmem, hbm],
            out_specs=[vmem, vmem],
            out_shape=(message(HI), shape((EXTRA, width), f32)),
            scratch_shapes=rows_of(HI),
            compiler_params=params,
            cost_estimate=cost(2 * macs, 1 << 20),
        )(order, came, pre_grad, total, w_first)

    from_left, from_right = right(begin(far, 0)), left(begin(far, 1))
    total_left, total_right = gate_mine, jnp.zeros_like(gate_mine)
    for d in range(far - 1, 0, -1):
        start = d == far - 1
        if d == 1:
            from_left, grad_down = lax.optimization_barrier((from_left, grad_down))
        go_right, total_left = carry_on(d, 0 if start else None, from_left, total_left)
        go_left, total_right = carry_on(-d, 1 if start else None, from_right, total_right)
        from_left, from_right = right(go_right), left(go_left)
    up_early = up_call(
        functools.partial(up_kernel, near, False),
        in_specs=[smem, vmem, vmem, vmem],
        scratch_shapes=rows_of(len(near) * HI),
    )(order_x, x_near, x_near_other, pre_grad)
    from_left, up_early, x_rest_other = lax.optimization_barrier(
        (from_left, up_early, x_rest_other)
    )
    grad_up = up_call(
        functools.partial(up_kernel, rest, True),
        in_specs=[smem, vmem, vmem, vmem, hbm],
        input_output_aliases={4: 0},
        scratch_shapes=rows_of(len(rest) * HI),
    )(order_x, x_rest, x_rest_other, pre_grad, up_early)
    n_gate = capacity // width
    summed, gate_half = pl.pallas_call(
        last_kernel,
        in_specs=[smem, vmem, vmem, vmem, vmem, vmem, hbm],
        out_specs=[vmem, vmem],
        out_shape=(shape((HI, capacity, width), bf16), shape((n_gate, width), f32)),
        scratch_shapes=rows_of(HI),
        compiler_params=params,
        cost_estimate=cost(2 * macs, 2 << 20),
    )(order, from_left, from_right, pre_grad, total_left, total_right, w_first)
    gate_total = gate_half + lax.ppermute(gate_half, "hi", [(0, 1), (1, 0)])
    returned = lax.all_to_all(
        summed.reshape(HI * n_experts, n_slots, width), ("hi", "ep"), 0, 0, tiled=True
    ).reshape(HI, capacity, width)

    grad_tokens = pl.pallas_call(
        combine_kernel,
        out_shape=shape((n_tokens, width), bf16),
        compiler_params=params,
    )(selector, returned)
    return grad_tokens, grad_up[None], grad_down[None], gate_total.reshape(1, capacity)


def solution(mesh):
    n_ep, n_et = mesh.devices.shape
    fine = Mesh(mesh.devices.reshape(n_ep, HI, n_et // HI), ("ep", "hi", "row"))
    et = ("hi", "row")
    in_specs = (
        P("ep", et),
        P("ep", et),
        P("ep", None, et),
        P("ep", et, None),
        P("ep", None, et),
        P("ep", None),
        P("ep", None, None),
        P("ep", None),
    )
    out_specs = (P("ep", et), P("ep", None, et), P("ep", et, None), P("ep", None))
    return jax.shard_map(
        per_device, mesh=fine, in_specs=in_specs, out_specs=out_specs, check_vma=False
    )
```

```python
import functools

import jax
import jax.numpy as jnp
from jax import lax
from jax.experimental import pallas as pl
from jax.experimental.pallas import tpu as pltpu
from jax.sharding import Mesh, PartitionSpec as P

HI = 2
EXTRA = 16
NN = (((1,), (0,)), ((), ()))
NT = (((1,), (1,)), ((), ()))
TN = (((0,), (0,)), ((), ()))
VMEM_LIMIT = 12 << 20


def dot32(a, b, dims=NN):
    return lax.dot_general(a, b, dims, preferred_element_type=jnp.float32)


def pick_kernel(picks_ref, counts_ref, tokens_ref, cotangent_ref, sel_ref, out_ref):
    n_slots, n_experts = picks_ref.shape
    n_tokens = tokens_ref.shape[0]
    slot = lax.broadcasted_iota(jnp.int32, (n_slots, n_experts), 0)
    wanted = jnp.where(slot < counts_ref[...], picks_ref[...], -1)
    positions = lax.broadcasted_iota(jnp.int32, (n_slots, n_tokens), 1)
    for e in range(n_experts):
        hit = wanted[:, e : e + 1] == positions
        sel_ref[e * n_slots : (e + 1) * n_slots, :] = hit.astype(jnp.float32).astype(
            jnp.bfloat16
        )
    both = jnp.concatenate([tokens_ref[...], cotangent_ref[...]], axis=1)
    picked = dot32(sel_ref[...], both).astype(jnp.bfloat16)
    for h in range(HI):
        out_ref[h] = picked


def place(order_ref, h, d):
    n_rows = order_ref.shape[0] // HI
    return pl.multiple_of(order_ref[h * n_rows + d % n_rows] * 128, 128)


def y_of(blocks, h):
    return blocks[0][2 * h] if len(blocks) == 1 else blocks[h][0]


def pack_kernel(hi_ref, arrived_ref, out_ref):
    width = out_ref.shape[-1]
    out_ref[0] = arrived_ref[0, :, width:]
    out_ref[1] = arrived_ref[hi_ref[0], :, :width]
    out_ref[2] = arrived_ref[1, :, width:]


def stack_kernel(*refs):
    for k, ref in enumerate(refs[:-1]):
        refs[-1][k] = ref[0]


def grouped(refs, distances, n_rows):
    groups, at = [], 0
    for d in distances:
        count = 2 if d == n_rows // 2 else 1
        groups.append(refs[at : at + count])
        at += count
    return groups, refs[at:]


def load_columns(order_ref, source, target, sems, distances, axis):
    copies = []
    for k, d in enumerate(distances):
        for h in range(HI):
            at = pl.ds(place(order_ref, h, d), 128)
            to = pl.ds((k * HI + h) * 128, 128)
            copies.append(
                pltpu.make_async_copy(
                    source.at[:, at] if axis else source.at[at],
                    target.at[:, to] if axis else target.at[to],
                    sems.at[k * HI + h],
                )
            )
            copies[-1].start()
    return copies


def back_kernel(distances, n_rows, last, order_ref, *refs):
    groups, rest = grouped(refs, distances, n_rows)
    if last:
        down_hbm, before_ref, pre_ref, gate_ref, pre_grad_ref, gate_out, down, sems = rest
    else:
        down_hbm, back_ref, down, sems = rest
    copies = load_columns(order_ref, down_hbm, down, sems, distances, 1)
    back = before_ref[...] if last else None
    for k in range(len(distances)):
        for h in range(HI):
            copies[k * HI + h].wait()
        pair = jnp.concatenate(
            [y_of(groups[k], h) for h in range(HI)], axis=1
        )
        term = dot32(pair, down[:, k * HI * 128 : (k + 1) * HI * 128], NT)
        back = term if back is None else back + term
    if not last:
        back_ref[...] = back
        return
    act = pre_ref[...].astype(jnp.float32)
    pre_grad_ref[...] = jnp.where(act > 0, gate_ref[...] * back, 0.0).astype(jnp.bfloat16)
    capacity, units = act.shape
    row_sum = lax.dot_general(
        jnp.ones((8, units), jnp.float32),
        jnp.maximum(act, 0.0) * back,
        NT,
        precision=lax.Precision.HIGHEST,
        preferred_element_type=jnp.float32,
    )
    rows = lax.broadcasted_iota(jnp.int32, (8, 128), 0)
    n_gate = capacity // 128
    packed = jnp.zeros((8, 128), jnp.float32)
    for k in range(n_gate):
        packed = jnp.where(
            rows % n_gate == k, row_sum[:, k * 128 : (k + 1) * 128], packed
        )
    high = packed.astype(jnp.bfloat16).astype(jnp.float32)
    packed = jnp.where(rows < n_gate, high, packed - high)
    gate_out[...] = jnp.concatenate([packed, jnp.zeros_like(packed)], axis=0)


def own_parts(order_ref, pre_grad_ref, up_hbm, up, sems, wanted):
    copies = []
    for k, (d, h) in enumerate(wanted):
        copies.append(
            pltpu.make_async_copy(
                up_hbm.at[pl.ds(place(order_ref, h, d), 128)],
                up.at[pl.ds(k * 128, 128)],
                sems.at[k],
            )
        )
        copies[-1].start()
    for copy in copies:
        copy.wait()
    parts = dot32(pre_grad_ref[...], up[...], NT)
    return [parts[:, k * 128 : (k + 1) * 128] for k in range(len(wanted))]


def first_kernel(d, h, order_ref, pre_grad_ref, gate_ref, up_hbm, out_ref, up, sems):
    (part,) = own_parts(order_ref, pre_grad_ref, up_hbm, up, sems, [(d, h)])
    capacity = pre_grad_ref.shape[0]
    out_ref[0, :capacity, :] = part.astype(jnp.bfloat16)
    out_ref[0, capacity:, :] = gate_ref[...].astype(jnp.bfloat16)


def pass_kernel(
    d, only, order_ref, came, pre_grad_ref, total_ref, up_hbm, out_ref, total_out, up, sems
):
    parts = own_parts(order_ref, pre_grad_ref, up_hbm, up, sems, [(d, 0), (d, 1)])
    capacity = pre_grad_ref.shape[0]
    for h in range(HI):
        part = parts[h]
        if only is None:
            part = part + came[h, :capacity, :].astype(jnp.float32)
        elif h == only:
            part = part + came[0, :capacity, :].astype(jnp.float32)
        out_ref[h, :capacity, :] = part.astype(jnp.bfloat16)
        out_ref[h, capacity:, :] = came[0, capacity:, :]
    total_out[...] = total_ref[...] + came[0, capacity:, :].astype(jnp.float32)


def last_kernel(
    order_ref, from_left, from_right, pre_grad_ref, total_left, total_right, up_hbm,
    sum_ref, gate_out, up, sems,
):
    parts = own_parts(order_ref, pre_grad_ref, up_hbm, up, sems, [(0, 0), (0, 1)])
    capacity = pre_grad_ref.shape[0]
    for h in range(HI):
        sum_ref[h] = (
            parts[h]
            + from_left[h, :capacity, :].astype(jnp.float32)
            + from_right[h, :capacity, :].astype(jnp.float32)
        ).astype(jnp.bfloat16)
    n_gate = capacity // 128
    total = total_left[...] + total_right[...] + from_left[0, capacity:, :].astype(jnp.float32)
    gate_out[...] = total[:n_gate] + total[n_gate : 2 * n_gate]


def down_kernel(distances, n_rows, more, order_ref, *refs):
    groups, rest = grouped(refs, distances, n_rows)
    if more:
        pre_ref, gate_ref, _, out_hbm, out, sems = rest
    else:
        pre_ref, gate_ref, out_hbm, out, sems = rest
    hidden_t = jnp.maximum(pre_ref[...].astype(jnp.float32), 0.0).T.astype(jnp.bfloat16)
    copies = []
    for k, d in enumerate(distances):
        pair = jnp.concatenate(
            [y_of(groups[k], h) for h in range(HI)], axis=1
        )
        scaled = (gate_ref[...] * pair.astype(jnp.float32)).astype(jnp.bfloat16)
        out[:, k * HI * 128 : (k + 1) * HI * 128] = dot32(hidden_t, scaled).astype(
            jnp.bfloat16
        )
        for h in range(HI):
            copies.append(
                pltpu.make_async_copy(
                    out.at[:, pl.ds((k * HI + h) * 128, 128)],
                    out_hbm.at[:, pl.ds(place(order_ref, h, d), 128)],
                    sems.at[k * HI + h],
                )
            )
            copies[-1].start()
    for copy in copies:
        copy.wait()


def up_kernel(distances, more, order_ref, own_ref, other_ref, pre_grad_ref, *refs):
    out_hbm, out, sems = refs[1:] if more else refs
    copies = []
    for k, d in enumerate(distances):
        pair = jnp.concatenate([own_ref[k], other_ref[k]], axis=1)
        out[k * HI * 128 : (k + 1) * HI * 128, :] = dot32(
            pair, pre_grad_ref[...], TN
        ).astype(jnp.bfloat16)
        for h in range(HI):
            copies.append(
                pltpu.make_async_copy(
                    out.at[pl.ds((k * HI + h) * 128, 128)],
                    out_hbm.at[pl.ds(place(order_ref, h, d), 128)],
                    sems.at[k * HI + h],
                )
            )
            copies[-1].start()
    for copy in copies:
        copy.wait()


def combine_kernel(sel_ref, returned_ref, out_ref):
    both = jnp.concatenate([returned_ref[h] for h in range(HI)], axis=1)
    total = dot32(sel_ref[...], both, TN)
    width = out_ref.shape[1]
    out_ref[...] = (total[:, :width] + total[:, width:]).astype(jnp.bfloat16)


def cost(flops, nbytes):
    return pl.CostEstimate(flops=flops, bytes_accessed=nbytes, transcendentals=0)


def per_device(tokens, cotangent, w_up, w_down, saved_pre, gates, picks, counts):
    bf16, f32 = jnp.bfloat16, jnp.float32
    n_tokens, width = tokens.shape
    _, n_experts, n_slots = picks.shape
    _, d_model, units = w_up.shape
    capacity = n_experts * n_slots
    n_rows = d_model // width // HI
    far = n_rows // 2
    macs = capacity * units * width * HI
    params = pltpu.CompilerParams(vmem_limit_bytes=VMEM_LIMIT)
    shape = jax.ShapeDtypeStruct
    hbm = pl.BlockSpec(memory_space=pl.ANY)
    vmem = pl.BlockSpec(memory_space=pltpu.VMEM)
    smem = pl.BlockSpec(memory_space=pltpu.SMEM)
    dma = pltpu.SemaphoreType.DMA

    def right(a):
        return lax.ppermute(a, "row", [(i, (i + 1) % n_rows) for i in range(n_rows)])

    def left(a):
        return lax.ppermute(a, "row", [(i, (i - 1) % n_rows) for i in range(n_rows)])

    hi, row = lax.axis_index("hi"), lax.axis_index("row")
    ahead_of = (row + jnp.arange(n_rows, dtype=jnp.int32)) % n_rows
    order = jnp.concatenate([h * n_rows + ahead_of for h in range(HI)])
    order_x = jnp.concatenate([h * n_rows + ahead_of for h in (hi, 1 - hi)])
    gate_column = gates[0][:, None]
    pre, w_first, w_second = saved_pre[0], w_up[0], w_down[0]

    selector, picked = pl.pallas_call(
        pick_kernel,
        out_shape=(
            shape((capacity, n_tokens), bf16),
            shape((HI, capacity, 2 * width), bf16),
        ),
    )(picks[0].T, counts, tokens, cotangent)
    arrived = lax.all_to_all(
        picked.reshape(HI * n_experts, n_slots, 2 * width), ("hi", "ep"), 0, 0, tiled=True
    ).reshape(HI, capacity, 2 * width)

    arrived, order, order_x, gate_column = lax.optimization_barrier(
        (arrived, order, order_x, gate_column)
    )
    packed = pl.pallas_call(
        pack_kernel,
        in_specs=[smem, vmem],
        out_specs=vmem,
        out_shape=shape((HI + 1, capacity, width), bf16),
        compiler_params=params,
    )(hi[None], arrived)

    def stacked(pieces):
        return pl.pallas_call(
            stack_kernel,
            grid=(1,),
            in_specs=[pl.BlockSpec((1, capacity, width), lambda i: (1, 0, 0))]
            * len(pieces),
            out_specs=pl.BlockSpec((len(pieces), capacity, width), lambda i: (0, 0, 0)),
            out_shape=shape((len(pieces), capacity, width), bf16),
            compiler_params=params,
            cost_estimate=cost(0, 2 << 20),
        )(*pieces)

    def crossed(a):
        return lax.ppermute(a, "hi", [(0, 1), (1, 0)])

    blocks = {0: [packed]}
    behind = ahead = packed
    near = (0, 1, -1)
    for d in range(1, far):
        ahead, behind = left(ahead), right(behind)
        blocks[d], blocks[-d] = [ahead], [behind]
        if d == 1:
            x_near = stacked([blocks[k][0] for k in near])
            x_near_other = crossed(x_near)
    late = [1 - far, far - 1, far]
    early = [d for d in blocks if d not in late]
    flat = lambda distances: [b for d in distances for b in blocks[d]]
    columns = lambda n: [pltpu.VMEM((units, n * HI * width), bf16), dma((n * HI,))]
    rows_of = lambda n: [pltpu.VMEM((n * width, units), bf16), dma((n,))]

    back = pl.pallas_call(
        functools.partial(back_kernel, early, n_rows, False),
        in_specs=[smem] + [vmem] * len(flat(early)) + [hbm],
        out_specs=vmem,
        out_shape=shape((capacity, units), f32),
        scratch_shapes=columns(len(early)),
        compiler_params=params,
        cost_estimate=cost(2 * macs * len(early), 4 << 20),
    )(order, *flat(early), w_second)
    down_early = pl.pallas_call(
        functools.partial(down_kernel, early, n_rows, False),
        in_specs=[smem] + [vmem] * (len(flat(early)) + 2),
        out_specs=hbm,
        out_shape=shape((units, d_model), bf16),
        scratch_shapes=columns(len(early)),
        compiler_params=params,
        cost_estimate=cost(2 * macs * len(early), 4 << 20),
    )(order, *flat(early), pre, gate_column)
    ahead, behind, back, down_early, x_near_other = lax.optimization_barrier(
        (ahead, behind, back, down_early, x_near_other)
    )
    blocks[1 - far], blocks[far - 1] = [behind], [ahead]
    blocks[far] = [right(behind[:2]), left(ahead[2:])]
    rest = [d for d in blocks if d not in near]
    x_rest = stacked([blocks[d][0] for d in rest])
    x_rest_other = crossed(x_rest)
    pre_grad, gate_mine = pl.pallas_call(
        functools.partial(back_kernel, late, n_rows, True),
        in_specs=[smem] + [vmem] * len(flat(late)) + [hbm, vmem, vmem, vmem],
        out_specs=[vmem, vmem],
        out_shape=(shape((capacity, units), bf16), shape((EXTRA, width), f32)),
        scratch_shapes=columns(len(late)),
        compiler_params=params,
        cost_estimate=cost(2 * macs * len(late), 3 << 20),
    )(order, *flat(late), w_second, back, pre, gate_column)

    grad_down = pl.pallas_call(
        functools.partial(down_kernel, late, n_rows, True),
        in_specs=[smem] + [vmem] * (len(flat(late)) + 2) + [hbm],
        out_specs=hbm,
        out_shape=shape((units, d_model), bf16),
        input_output_aliases={len(flat(late)) + 3: 0},
        scratch_shapes=columns(len(late)),
        compiler_params=params,
        cost_estimate=cost(2 * macs * len(late), 3 << 20),
    )(order, *flat(late), pre, gate_column, down_early)
    up_call = functools.partial(
        pl.pallas_call,
        out_specs=hbm,
        out_shape=shape((d_model, units), bf16),
        compiler_params=params,
        cost_estimate=cost(2 * macs * 4, 4 << 20),
    )
    message = lambda n: shape((n, capacity + EXTRA, width), bf16)
    def begin(d, h):
        return pl.pallas_call(
            functools.partial(first_kernel, d, h),
            in_specs=[smem, vmem, vmem, hbm],
            out_specs=vmem,
            out_shape=message(1),
            scratch_shapes=rows_of(1),
            compiler_params=params,
            cost_estimate=cost(macs, 1 << 20),
        )(order, pre_grad, gate_mine, w_first)

    def carry_on(d, only, came, total):
        return pl.pallas_call(
            functools.partial(pass_kernel, d, only),
            in_specs=[smem, vmem, vmem, vmem, hbm],
            out_specs=[vmem, vmem],
            out_shape=(message(HI), shape((EXTRA, width), f32)),
            scratch_shapes=rows_of(HI),
            compiler_params=params,
            cost_estimate=cost(2 * macs, 1 << 20),
        )(order, came, pre_grad, total, w_first)

    from_left, from_right = right(begin(far, 0)), left(begin(far, 1))
    total_left, total_right = gate_mine, jnp.zeros_like(gate_mine)
    for d in range(far - 1, 0, -1):
        start = d == far - 1
        if d == 1:
            from_left, grad_down = lax.optimization_barrier((from_left, grad_down))
        go_right, total_left = carry_on(d, 0 if start else None, from_left, total_left)
        go_left, total_right = carry_on(-d, 1 if start else None, from_right, total_right)
        from_left, from_right = right(go_right), left(go_left)
    up_early = up_call(
        functools.partial(up_kernel, near, False),
        in_specs=[smem, vmem, vmem, vmem],
        scratch_shapes=rows_of(len(near) * HI),
    )(order_x, x_near, x_near_other, pre_grad)
    from_left, up_early, x_rest_other = lax.optimization_barrier(
        (from_left, up_early, x_rest_other)
    )
    grad_up = up_call(
        functools.partial(up_kernel, rest, True),
        in_specs=[smem, vmem, vmem, vmem, hbm],
        input_output_aliases={4: 0},
        scratch_shapes=rows_of(len(rest) * HI),
    )(order_x, x_rest, x_rest_other, pre_grad, up_early)
    n_gate = capacity // width
    summed, gate_half = pl.pallas_call(
        last_kernel,
        in_specs=[smem, vmem, vmem, vmem, vmem, vmem, hbm],
        out_specs=[vmem, vmem],
        out_shape=(shape((HI, capacity, width), bf16), shape((n_gate, width), f32)),
        scratch_shapes=rows_of(HI),
        compiler_params=params,
        cost_estimate=cost(2 * macs, 2 << 20),
    )(order, from_left, from_right, pre_grad, total_left, total_right, w_first)
    gate_total = gate_half + lax.ppermute(gate_half, "hi", [(0, 1), (1, 0)])
    returned = lax.all_to_all(
        summed.reshape(HI * n_experts, n_slots, width), ("hi", "ep"), 0, 0, tiled=True
    ).reshape(HI, capacity, width)

    grad_tokens = pl.pallas_call(
        combine_kernel,
        out_shape=shape((n_tokens, width), bf16),
        compiler_params=params,
    )(selector, returned)
    return grad_tokens, grad_up[None], grad_down[None], gate_total.reshape(1, capacity)


def solution(mesh):
    n_ep, n_et = mesh.devices.shape
    fine = Mesh(mesh.devices.reshape(n_ep, HI, n_et // HI), ("ep", "hi", "row"))
    et = ("hi", "row")
    in_specs = (
        P("ep", et),
        P("ep", et),
        P("ep", None, et),
        P("ep", et, None),
        P("ep", None, et),
        P("ep", None),
        P("ep", None, None),
        P("ep", None),
    )
    out_specs = (P("ep", et), P("ep", None, et), P("ep", et, None), P("ep", None))
    return jax.shard_map(
        per_device, mesh=fine, in_specs=in_specs, out_specs=out_specs, check_vma=False
    )
```
